32 devices in a mesh: wide: 16 (over z, y, x), narrow: 2 (over core).
Axes of the slice: x: 2, y: 2, z: 4, core: 2. Of those that a mesh axis runs over, the one named last changes fastest.
Arguments:
- amplitudes: bfloat16 [384, 512], P('wide', 'narrow'), may hold values from -6 to 6
- integrals: bfloat16 [262144, 512], P('wide', 'narrow'), may hold values from -0.75 to 0.75
- virtual_irrep: int32 [512], replicated, may hold values from 0 to 7
- column_irrep: int32 [512], P('narrow'), may hold values from 0 to 7
- pair_energy: float32 [384], P('narrow'), may hold values from -4 to -1
- virtual_energy: float32 [512], replicated, may hold values from 0.5 to 3
- residual_in: bfloat16 [384, 262144], P('narrow', 'wide'), may hold values from -6 to 6
Outputs:
- new_amplitudes: bfloat16 [384, 262144], P('narrow', 'wide')
The draws below stay inside these ranges and needn't reach their ends.
All inputs are finite; a program needn't handle non-finite values.
Results may differ from the reference program's by a relative error of at most 0.012.
Values may be sent and summed in bfloat16 or wider, within the bound.
A program may use at most 128 MiB of HBM per device.

```python
import jax
import jax.numpy as jnp
from jax import lax

NV = 512
NIRREP = 8
CD_DEV = 256
OO = 384
AB = 262144
CD = 512
N_NARROW = 2


def with_ends(array, rng, smallest, high):
    longest = array.shape.index(max(array.shape))
    spots = []
    for shift in (0, 1):
        where = [jax.random.randint(jax.random.fold_in(rng, axis), (), 0, length) for axis, length in enumerate(array.shape)]
        where[longest] = (where[longest] + shift) % array.shape[longest]
        spots.append(tuple(where))
    return array.at[spots[0]].set(smallest).at[spots[1]].set(high)


def shard_levels(key, shape, cuts, smallest, largest):
    loudness = 1.0
    for position, blocks in cuts:
        draws = jax.random.uniform(jax.random.fold_in(jax.random.fold_in(key, 6), position), (blocks,), jnp.float32, smallest / len(cuts), largest / len(cuts))
        loudness = loudness * jnp.repeat(jnp.exp(draws), shape[position] // blocks).reshape((-1,) + (1,) * (len(shape) - 1 - position))
    return loudness


def bell_draw(rng, extent, deviation, most, split=(), kind=jnp.bfloat16):
    result = deviation * jax.random.normal(rng, extent, jnp.float32)
    if split:
        result = result * shard_levels(rng, extent, split, -0.22, 0.18)
    return jnp.clip(result, -most, most).astype(kind)


def setup_inputs(seed: int = 0) -> dict:
    arg_keys = jax.random.split(jax.random.key(seed), 8)
    amplitudes = bell_draw(arg_keys[0], (OO, CD), 1.0, 6.0, ((0, 16), (1, 2)))
    integrals = bell_draw(arg_keys[1], (AB, CD), (CD // 8) ** -0.5, 0.75, ((0, 16), (1, 2)))
    virtual_irrep = with_ends(jax.random.randint(arg_keys[2], (NV,), 0, NIRREP), jax.random.fold_in(arg_keys[2], 1), 0, NIRREP - 1).astype(jnp.int32)
    column_irrep = with_ends(jax.random.randint(arg_keys[3], (CD,), 0, NIRREP), jax.random.fold_in(arg_keys[3], 1), 0, NIRREP - 1).astype(jnp.int32)
    pair_energy = jnp.clip(-4.0 + 3.0 * jax.random.uniform(arg_keys[4], (OO,), jnp.float32) ** shard_levels(arg_keys[4], (OO,), ((0, 2),), -0.2, 0.2), -4.0, -1.0)
    virtual_energy = jnp.clip(jax.random.uniform(arg_keys[5], (NV,), jnp.float32, 0.5, 3.0), 0.5, 3.0)
    residual_in = bell_draw(arg_keys[6], (OO, AB), 1.0, 6.0, ((0, 2), (1, 16)))
    return {"amplitudes": amplitudes, "integrals": integrals, "virtual_irrep": virtual_irrep, "column_irrep": column_irrep, "pair_energy": pair_energy, "virtual_energy": virtual_energy, "residual_in": residual_in}


def reference(amplitudes, integrals, virtual_irrep, column_irrep, pair_energy, virtual_energy, residual_in):
    amp_wide = amplitudes.astype(jnp.float32).reshape(OO, N_NARROW, CD_DEV)
    row_irrep = jnp.bitwise_xor(virtual_irrep[:, None], virtual_irrep[None, :]).reshape(NV * NV)
    block_size = 8 * NV
    block_count = NV // 8

    def block_ladder(index):
        offset = (index * block_size).astype(jnp.int32)
        rows_block = lax.dynamic_slice_in_dim(integrals, offset, block_size, 0)
        irrep_block = lax.dynamic_slice_in_dim(row_irrep, offset, block_size, 0)
        masked = jnp.where(irrep_block[:, None] == column_irrep[None, :], rows_block, jnp.zeros((), jnp.bfloat16))
        masked_wide = masked.astype(jnp.float32).reshape(block_size, N_NARROW, CD_DEV)
        partial_value = jnp.einsum('ogc,bgc->gob', amp_wide, masked_wide)
        rounded = lax.optimization_barrier(partial_value.astype(jnp.bfloat16))
        return jnp.sum(rounded.astype(jnp.float32), axis=0)

    ladder = lax.map(block_ladder, jnp.arange(block_count, dtype=jnp.int32))
    ladder = jnp.transpose(ladder, (1, 0, 2)).reshape(OO, NV, NV)
    mirrored = jnp.transpose(ladder, (0, 2, 1))
    denominator = pair_energy[:, None, None] - virtual_energy[None, :, None] - virtual_energy[None, None, :]
    total = residual_in.astype(jnp.float32).reshape(OO, NV, NV) + ladder - mirrored
    return (total / denominator).reshape(OO, NV * NV).astype(jnp.bfloat16)
```

```python
import functools

import jax
import jax.numpy as jnp
from jax import lax
from jax.experimental import pallas as pl
from jax.experimental.pallas import tpu as pltpu
from jax.sharding import PartitionSpec as P

SLOTS = 64
MESH = pl.DeviceIdType.MESH
BF16 = jnp.bfloat16
F32 = jnp.float32


def dense(
    amplitudes, integrals, virtual_irrep, column_irrep, pair_energy, virtual_energy, residual_in
):
    wide_size = lax.axis_size("wide")
    num_virt = virtual_irrep.shape[0]
    a_local = num_virt // wide_size
    first_a = lax.axis_index("wide") * a_local
    local_irrep = lax.dynamic_slice_in_dim(virtual_irrep, first_a, a_local, 0)
    row_irrep = jnp.bitwise_xor(local_irrep[:, None], virtual_irrep[None, :]).reshape(
        a_local * num_virt
    )
    masked = jnp.where(
        row_irrep[:, None] == column_irrep[None, :], integrals, jnp.zeros((), integrals.dtype)
    )
    contract = (((1,), (1,)), ((), ()))
    terms = lax.dot_general(
        lax.all_gather(amplitudes, "wide", axis=0, tiled=True),
        masked,
        contract,
        preferred_element_type=jnp.float32,
    )
    ladder = lax.psum_scatter(
        terms.astype(jnp.bfloat16), "narrow", scatter_dimension=0, tiled=True
    ).astype(jnp.float32)
    pair_rows = ladder.shape[0]
    ladder_cube = ladder.reshape(pair_rows, a_local, num_virt)
    swapped = lax.all_to_all(
        ladder_cube.astype(jnp.bfloat16), "wide", split_axis=2, concat_axis=2, tiled=True
    ).astype(ladder_cube.dtype)
    mirrored = swapped.reshape(pair_rows, a_local, wide_size, a_local)
    mirrored = jnp.transpose(mirrored, (0, 3, 2, 1)).reshape(pair_rows, a_local * num_virt)
    local_energy = lax.dynamic_slice_in_dim(virtual_energy, first_a, a_local, 0)
    denominator = (
        pair_energy[:, None, None] - local_energy[None, :, None] - virtual_energy[None, None, :]
    )
    denominator = denominator.reshape(pair_rows, a_local * num_virt)
    total = residual_in.astype(jnp.float32) + ladder - mirrored
    return (total / denominator).astype(jnp.bfloat16)


def partner(me, step, n):
    result, bit = 0, 1
    while bit < n:
        result += ((me // bit + step // bit) % 2) * bit
        bit *= 2
    return result


def exchange_kernel(
    n, v_ref, irb_ref, colx_ref, s_ref, lc_ref, rx_ref,
    vbuf, fbuf, tx, lcbuf, load_sem, send_sem, recv_sem, fsend_sem, frecv_sem, own_sem, lc_sem,
):
    me, core = lax.axis_index("wide"), lax.axis_index("narrow")
    other = 1 - core
    al = v_ref.shape[0]
    half = al // 2
    width = v_ref.shape[2]

    def load(i):
        to = partner(me, n - 1 - i, n)
        columns = pl.ds(pl.multiple_of(to * al, al), al)
        return pltpu.make_async_copy(v_ref.at[:, columns, :], vbuf.at[i], load_sem.at[i])

    def send(i):
        to = partner(me, n - 1 - i, n)
        return pltpu.make_async_remote_copy(
            src_ref=tx.at[i], dst_ref=rx_ref.at[core, me], send_sem=send_sem.at[i],
            recv_sem=recv_sem.at[i], device_id=(to, core), device_id_type=MESH,
        )

    def arrival(i):
        source = partner(me, n - 1 - i, n)
        return pltpu.make_async_remote_copy(
            src_ref=tx.at[i], dst_ref=rx_ref.at[core, source], send_sem=send_sem.at[i],
            recv_sem=recv_sem.at[i], device_id=(source, core), device_id_type=MESH,
        )

    def forward(i):
        source = partner(me, n - 1 - i, n)
        return pltpu.make_async_remote_copy(
            src_ref=rx_ref.at[core, source], dst_ref=rx_ref.at[core, source],
            send_sem=fsend_sem.at[i], recv_sem=frecv_sem.at[i],
            device_id=(me, other), device_id_type=MESH,
        )

    def forwarded(i):
        source = partner(me, n - 1 - i, n)
        return pltpu.make_async_remote_copy(
            src_ref=rx_ref.at[other, source], dst_ref=rx_ref.at[other, source],
            send_sem=fsend_sem.at[i], recv_sem=frecv_sem.at[i],
            device_id=(me, other), device_id_type=MESH,
        )

    barrier = pltpu.get_barrier_semaphore()

    @pl.loop(0, n - 1)
    def _(i):
        pl.semaphore_signal(
            barrier, inc=1, device_id=(partner(me, n - 1 - i, n), core), device_id_type=MESH
        )

    pl.semaphore_signal(barrier, inc=1, device_id=(me, other), device_id_type=MESH)

    @pl.loop(0, n)
    def _(i):
        load(i).start()

    pl.semaphore_wait(barrier, n)

    @pl.loop(0, n)
    def _(i):
        to = partner(me, n - 1 - i, n)
        load(i).wait()
        rows = irb_ref[pl.ds(pl.multiple_of(to * al, al), al), :]
        block = vbuf[i]
        masked = jnp.where(rows[None] == colx_ref[...], block, jnp.zeros_like(block))
        low, high = s_ref[0], s_ref[1]

        def pack(first, second):
            return jnp.dot(
                first.reshape(half * al, width), low, preferred_element_type=F32
            ) + jnp.dot(second.reshape(half * al, width), high, preferred_element_type=F32)

        fbuf[...] = pack(masked[:half], masked[half:])
        pairs = masked.reshape(half, 2, al, width)
        lcbuf[to] = pack(pairs[:, 0], pairs[:, 1]).astype(BF16).reshape(half, al, 2 * SLOTS)
        for b in range(al):
            tx[i, b] = fbuf[pl.ds(b, half, stride=al), :].astype(BF16)

        @pl.when(i < n - 1)
        def _():
            send(i).start()

    own = pltpu.make_async_copy(tx.at[n - 1], rx_ref.at[core, me], own_sem)
    own.start()
    keep = pltpu.make_async_copy(lcbuf, lc_ref.at[core], lc_sem.at[0])
    keep.start()
    give = pltpu.make_async_remote_copy(
        src_ref=lcbuf, dst_ref=lc_ref.at[core], send_sem=lc_sem.at[1], recv_sem=lc_sem.at[2],
        device_id=(me, other), device_id_type=MESH,
    )
    give.start()
    own.wait()
    forward(n - 1).start()

    @pl.loop(0, n - 1)
    def _(k):
        i = n - 2 - k
        arrival(i).wait_recv()
        forward(i).start()

    @pl.loop(0, n - 1)
    def _(i):
        send(i).wait_send()

    @pl.loop(0, n)
    def _(i):
        forward(i).wait_send()
        forwarded(i).wait_recv()

    keep.wait()
    give.wait_send()
    pltpu.make_async_remote_copy(
        src_ref=lcbuf, dst_ref=lc_ref.at[other], send_sem=lc_sem.at[1], recv_sem=lc_sem.at[2],
        device_id=(me, other), device_id_type=MESH,
    ).wait_recv()


def finish_kernel(
    lc_ref, rx_ref, w_ref, t_ref, colx_ref, irb_ref, res_ref, pe_ref, vsum_ref, out_ref, ebuf
):
    n, half, slots = rx_ref.shape[1], rx_ref.shape[3], rx_ref.shape[4]
    width = irb_ref.shape[1]
    num_virt = irb_ref.shape[0]
    irb = irb_ref[...].reshape(n, 2, half, width)
    for h in range(2):
        for core in range(2):
            mirror = rx_ref[core, :, h].reshape(n * half, slots)
            span = slice(core * width, (core + 1) * width)
            for bh in range(2):
                direct = lc_ref[core, :, 0, bh * half:(bh + 1) * half].reshape(n * half, slots)
                both = jnp.concatenate([direct, mirror], axis=1)
                spread = jnp.dot(both, w_ref[core, h, bh], preferred_element_type=F32)
                spread = spread.astype(BF16).reshape(n, half, width)
                mask = irb[:, bh] == colx_ref[h, :, span][None]
                ebuf[:, bh, :, span] = jnp.where(mask, spread, jnp.zeros_like(spread))
        ladder = lax.dot_general(
            t_ref[...], ebuf[...].reshape(num_virt, 2 * width),
            (((1,), (1,)), ((), ())), preferred_element_type=F32,
        )
        cols = slice(h * num_virt, (h + 1) * num_virt)
        total = res_ref[:, cols].astype(F32) + ladder
        out_ref[:, cols] = (total / (pe_ref[...] - vsum_ref[:, cols])).astype(BF16)


def ranks(column_irrep):
    same = column_irrep[:, None] == column_irrep[None, :]
    index = jnp.arange(column_irrep.shape[0])
    return jnp.sum(same & (index[None, :] < index[:, None]), axis=1, dtype=jnp.int32)


def local(
    amplitudes, integrals, virtual_irrep, column_irrep, pair_energy, virtual_energy, residual_in
):
    n = lax.axis_size("wide")
    num_virt, width = virtual_irrep.shape[0], column_irrep.shape[0]
    al, half = num_virt // n, num_virt // n // 2
    pairs = pair_energy.shape[0]
    me, core = lax.axis_index("wide"), lax.axis_index("narrow")
    first_a = me * al
    local_irrep = lax.dynamic_slice_in_dim(virtual_irrep, first_a, al, 0)

    amp_all = lax.all_gather(amplitudes, ("wide", "narrow"), axis=0)
    amp_all = amp_all.reshape(n, 2, amplitudes.shape[0], width)
    amp_all = lax.dynamic_slice_in_dim(amp_all, core * (n // 2), n // 2, 0)
    amp = jnp.transpose(amp_all, (0, 2, 1, 3)).reshape(pairs, 2 * width)
    columns = lax.all_gather(column_irrep, "narrow", axis=0)

    rank = ranks(column_irrep)
    slot = jnp.arange(2 * SLOTS)
    shift = jnp.array([0, SLOTS])[:, None, None]
    inside = (slot >= shift) & (slot < shift + SLOTS)
    pick = ((rank[None, :, None] + shift == slot) & inside).astype(BF16)
    colx = (local_irrep[:, None] ^ column_irrep[None, :]).astype(BF16)[:, None, :]
    irb = jnp.broadcast_to(virtual_irrep.astype(BF16)[:, None], (num_virt, width))

    vmem = pl.BlockSpec(memory_space=pltpu.VMEM)
    hbm = pl.BlockSpec(memory_space=pl.ANY)
    lc, rx = pl.pallas_call(
        functools.partial(exchange_kernel, n),
        out_shape=(
            jax.ShapeDtypeStruct((2, n, half, al, 2 * SLOTS), BF16),
            jax.ShapeDtypeStruct((2, n, al, half, 2 * SLOTS), BF16),
        ),
        in_specs=[hbm, vmem, vmem, vmem],
        out_specs=(hbm, hbm),
        scratch_shapes=[
            pltpu.VMEM((n, al, al, width), BF16),
            pltpu.VMEM((half * al, 2 * SLOTS), F32),
            pltpu.VMEM((n, al, half, 2 * SLOTS), BF16),
            pltpu.VMEM((n, half, al, 2 * SLOTS), BF16),
            pltpu.SemaphoreType.DMA((n,)),
            pltpu.SemaphoreType.DMA((n,)),
            pltpu.SemaphoreType.DMA((n,)),
            pltpu.SemaphoreType.DMA((n,)),
            pltpu.SemaphoreType.DMA((n,)),
            pltpu.SemaphoreType.DMA,
            pltpu.SemaphoreType.DMA((3,)),
        ],
        compiler_params=pltpu.CompilerParams(
            collective_id=0, has_side_effects=True, vmem_limit_bytes=40 * 2**20
        ),
        cost_estimate=pl.CostEstimate(
            flops=4 * al * num_virt * width * 2 * SLOTS,
            bytes_accessed=200 * 2**20, transcendentals=0,
        ),
    )(integrals.reshape(al, num_virt, width), irb, colx, pick)

    rank_all = jax.vmap(ranks)(columns)
    fits = jnp.max(rank_all) < SLOTS
    spread = (
        (rank_all[:, None, None, :] + shift[None] == slot[None, None, :, None])
        & jnp.swapaxes(inside, 1, 2)[None]
    )
    spread = spread.astype(BF16)
    shape = (2, 2, 2, 2 * SLOTS, width)
    weights = jnp.concatenate(
        [jnp.broadcast_to(spread[:, :, None], shape), jnp.broadcast_to(-spread[:, None], shape)],
        axis=3,
    )
    colx_all = (local_irrep[:, None] ^ columns.reshape(1, 2 * width)).astype(BF16)[:, None, :]
    local_energy = lax.dynamic_slice_in_dim(virtual_energy, first_a, al, 0)
    vsum = (local_energy[:, None] + virtual_energy[None, :]).reshape(1, al * num_virt)

    def short():
        whole = lambda *shape: pl.BlockSpec(shape, lambda p: (0,) * len(shape))
        return pl.pallas_call(
            finish_kernel,
            grid=(half,),
            out_shape=jax.ShapeDtypeStruct(residual_in.shape, BF16),
            in_specs=[
                pl.BlockSpec((2, n, 1, al, 2 * SLOTS), lambda p: (0, 0, p, 0, 0)),
                pl.BlockSpec((2, n, 2, half, 2 * SLOTS), lambda p: (0, 0, p, 0, 0)),
                whole(2, 2, 2, 4 * SLOTS, width),
                whole(pairs, 2 * width),
                pl.BlockSpec((2, 1, 2 * width), lambda p: (p, 0, 0)),
                whole(num_virt, width),
                pl.BlockSpec((pairs, 2 * num_virt), lambda p: (0, p)),
                whole(pairs, 1),
                pl.BlockSpec((1, 2 * num_virt), lambda p: (0, p)),
            ],
            out_specs=pl.BlockSpec((pairs, 2 * num_virt), lambda p: (0, p)),
            scratch_shapes=[pltpu.VMEM((n, 2, half, 2 * width), BF16)],
            compiler_params=pltpu.CompilerParams(vmem_limit_bytes=40 * 2**20),
        )(lc, rx, weights, amp, colx_all, irb, residual_in, pair_energy[:, None], vsum)

    def full():
        return dense(
            amplitudes, integrals, virtual_irrep, column_irrep, pair_energy, virtual_energy,
            residual_in,
        )

    return lax.cond(fits, short, full)


def solution(mesh):
    usable = mesh.shape["narrow"] == 2 and mesh.shape["wide"] == 16
    return jax.shard_map(
        local if usable else dense,
        mesh=mesh,
        in_specs=(
            P("wide", "narrow"),
            P("wide", "narrow"),
            P(),
            P("narrow"),
            P("narrow"),
            P(),
            P("narrow", "wide"),
        ),
        out_specs=P("narrow", "wide"),
        check_vma=False,
    )
```

```python
import functools

import jax
import jax.numpy as jnp
from jax import lax
from jax.experimental import pallas as pl
from jax.experimental.pallas import tpu as pltpu
from jax.sharding import PartitionSpec as P

SLOTS = 64
MESH = pl.DeviceIdType.MESH
BF16 = jnp.bfloat16
F32 = jnp.float32


def dense(
    amplitudes, integrals, virtual_irrep, column_irrep, pair_energy, virtual_energy, residual_in
):
    wide_size = lax.axis_size("wide")
    num_virt = virtual_irrep.shape[0]
    a_local = num_virt // wide_size
    first_a = lax.axis_index("wide") * a_local
    local_irrep = lax.dynamic_slice_in_dim(virtual_irrep, first_a, a_local, 0)
    row_irrep = jnp.bitwise_xor(local_irrep[:, None], virtual_irrep[None, :]).reshape(
        a_local * num_virt
    )
    masked = jnp.where(
        row_irrep[:, None] == column_irrep[None, :], integrals, jnp.zeros((), integrals.dtype)
    )
    contract = (((1,), (1,)), ((), ()))
    terms = lax.dot_general(
        lax.all_gather(amplitudes, "wide", axis=0, tiled=True),
        masked,
        contract,
        preferred_element_type=jnp.float32,
    )
    ladder = lax.psum_scatter(
        terms.astype(jnp.bfloat16), "narrow", scatter_dimension=0, tiled=True
    ).astype(jnp.float32)
    pair_rows = ladder.shape[0]
    ladder_cube = ladder.reshape(pair_rows, a_local, num_virt)
    swapped = lax.all_to_all(
        ladder_cube.astype(jnp.bfloat16), "wide", split_axis=2, concat_axis=2, tiled=True
    ).astype(ladder_cube.dtype)
    mirrored = swapped.reshape(pair_rows, a_local, wide_size, a_local)
    mirrored = jnp.transpose(mirrored, (0, 3, 2, 1)).reshape(pair_rows, a_local * num_virt)
    local_energy = lax.dynamic_slice_in_dim(virtual_energy, first_a, a_local, 0)
    denominator = (
        pair_energy[:, None, None] - local_energy[None, :, None] - virtual_energy[None, None, :]
    )
    denominator = denominator.reshape(pair_rows, a_local * num_virt)
    total = residual_in.astype(jnp.float32) + ladder - mirrored
    return (total / denominator).astype(jnp.bfloat16)


def partner(me, step, n):
    result, bit = 0, 1
    while bit < n:
        result += ((me // bit + step // bit) % 2) * bit
        bit *= 2
    return result


def exchange_kernel(
    n, v_ref, irb_ref, colx_ref, s_ref, amp_ref, lc_ref, rx_ref, t_ref,
    vbuf, fbuf, tx, lcbuf, tbuf, tsend_sem, trecv_sem, tgive_sem, load_sem, send_sem, recv_sem, fsend_sem, frecv_sem, own_sem, lc_sem,
):
    me, core = lax.axis_index("wide"), lax.axis_index("narrow")
    other = 1 - core
    al = v_ref.shape[0]
    half = al // 2
    width = v_ref.shape[2]

    def load(i):
        to = partner(me, n - 1 - i, n)
        columns = pl.ds(pl.multiple_of(to * al, al), al)
        return pltpu.make_async_copy(v_ref.at[:, columns, :], vbuf.at[i], load_sem.at[i])

    def send(i):
        to = partner(me, n - 1 - i, n)
        return pltpu.make_async_remote_copy(
            src_ref=tx.at[i], dst_ref=rx_ref.at[core, me], send_sem=send_sem.at[i],
            recv_sem=recv_sem.at[i], device_id=(to, core), device_id_type=MESH,
        )

    def arrival(i):
        source = partner(me, n - 1 - i, n)
        return pltpu.make_async_remote_copy(
            src_ref=tx.at[i], dst_ref=rx_ref.at[core, source], send_sem=send_sem.at[i],
            recv_sem=recv_sem.at[i], device_id=(source, core), device_id_type=MESH,
        )

    def forward(i):
        source = partner(me, n - 1 - i, n)
        return pltpu.make_async_remote_copy(
            src_ref=rx_ref.at[core, source], dst_ref=rx_ref.at[core, source],
            send_sem=fsend_sem.at[i], recv_sem=frecv_sem.at[i],
            device_id=(me, other), device_id_type=MESH,
        )

    def forwarded(i):
        source = partner(me, n - 1 - i, n)
        return pltpu.make_async_remote_copy(
            src_ref=rx_ref.at[other, source], dst_ref=rx_ref.at[other, source],
            send_sem=fsend_sem.at[i], recv_sem=frecv_sem.at[i],
            device_id=(me, other), device_id_type=MESH,
        )

    def send_amp(i):
        return pltpu.make_async_remote_copy(
            src_ref=amp_ref, dst_ref=tbuf.at[me], send_sem=tsend_sem.at[i],
            recv_sem=trecv_sem.at[i], device_id=(partner(me, n - 1 - i, n), core),
            device_id_type=MESH,
        )

    def arrived_amp(i):
        source = partner(me, n - 1 - i, n)
        return pltpu.make_async_remote_copy(
            src_ref=amp_ref, dst_ref=tbuf.at[source], send_sem=tsend_sem.at[i],
            recv_sem=trecv_sem.at[i], device_id=(source, core), device_id_type=MESH,
        )

    barrier = pltpu.get_barrier_semaphore()

    @pl.loop(0, n - 1)
    def _(i):
        pl.semaphore_signal(
            barrier, inc=1, device_id=(partner(me, n - 1 - i, n), core), device_id_type=MESH
        )

    pl.semaphore_signal(barrier, inc=1, device_id=(me, other), device_id_type=MESH)

    @pl.loop(0, n)
    def _(i):
        load(i).start()

    own_amp = pltpu.make_async_copy(amp_ref, tbuf.at[me], own_sem.at[1])
    own_amp.start()
    pl.semaphore_wait(barrier, n)

    @pl.loop(0, n - 1)
    def _(i):
        send_amp(i).start()

    @pl.loop(0, n)
    def _(i):
        to = partner(me, n - 1 - i, n)
        load(i).wait()
        rows = irb_ref[pl.ds(pl.multiple_of(to * al, al), al), :]
        block = vbuf[i]
        masked = jnp.where(rows[None] == colx_ref[...], block, jnp.zeros_like(block))
        low, high = s_ref[0], s_ref[1]

        def pack(first, second):
            return jnp.dot(
                first.reshape(half * al, width), low, preferred_element_type=F32
            ) + jnp.dot(second.reshape(half * al, width), high, preferred_element_type=F32)

        fbuf[...] = pack(masked[:half], masked[half:])
        pairs = masked.reshape(half, 2, al, width)
        lcbuf[to] = pack(pairs[:, 0], pairs[:, 1]).astype(BF16).reshape(half, al, 2 * SLOTS)
        for b in range(al):
            tx[i, b] = fbuf[pl.ds(b, half, stride=al), :].astype(BF16)

        @pl.when(i < n - 1)
        def _():
            send(i).start()

    own = pltpu.make_async_copy(tx.at[n - 1], rx_ref.at[core, me], own_sem.at[0])
    own.start()
    keep = pltpu.make_async_copy(lcbuf, lc_ref.at[core], lc_sem.at[0])
    keep.start()
    give = pltpu.make_async_remote_copy(
        src_ref=lcbuf, dst_ref=lc_ref.at[core], send_sem=lc_sem.at[1], recv_sem=lc_sem.at[2],
        device_id=(me, other), device_id_type=MESH,
    )
    give.start()
    own.wait()
    forward(n - 1).start()
    own_amp.wait()

    @pl.loop(0, n - 1)
    def _(i):
        arrived_amp(i).wait_recv()

    keep_amp = pltpu.make_async_copy(
        tbuf.at[pl.ds(core * (n // 2), n // 2)], t_ref.at[core], tgive_sem.at[0]
    )
    keep_amp.start()
    give_amp = pltpu.make_async_remote_copy(
        src_ref=tbuf.at[pl.ds(other * (n // 2), n // 2)], dst_ref=t_ref.at[core],
        send_sem=tgive_sem.at[1], recv_sem=tgive_sem.at[2],
        device_id=(me, other), device_id_type=MESH,
    )
    give_amp.start()

    @pl.loop(0, n - 1)
    def _(k):
        i = n - 2 - k
        arrival(i).wait_recv()
        forward(i).start()

    @pl.loop(0, n - 1)
    def _(i):
        send(i).wait_send()
        send_amp(i).wait_send()

    @pl.loop(0, n)
    def _(i):
        forward(i).wait_send()
        forwarded(i).wait_recv()

    keep_amp.wait()
    give_amp.wait_send()
    pltpu.make_async_remote_copy(
        src_ref=tbuf.at[pl.ds(other * (n // 2), n // 2)], dst_ref=t_ref.at[other],
        send_sem=tgive_sem.at[1], recv_sem=tgive_sem.at[2],
        device_id=(me, other), device_id_type=MESH,
    ).wait_recv()
    keep.wait()
    give.wait_send()
    pltpu.make_async_remote_copy(
        src_ref=lcbuf, dst_ref=lc_ref.at[other], send_sem=lc_sem.at[1], recv_sem=lc_sem.at[2],
        device_id=(me, other), device_id_type=MESH,
    ).wait_recv()


def finish_kernel(
    lc_ref, rx_ref, w_ref, t_ref, colx_ref, irb_ref, res_ref, pe_ref, vsum_ref, out_ref, ebuf
):
    n, half, slots = rx_ref.shape[1], rx_ref.shape[3], rx_ref.shape[4]
    width = irb_ref.shape[1]
    num_virt = irb_ref.shape[0]
    irb = irb_ref[...].reshape(n, 2, half, width)
    for h in range(2):
        for core in range(2):
            mirror = rx_ref[core, :, h].reshape(n * half, slots)
            span = slice(core * width, (core + 1) * width)
            for bh in range(2):
                direct = lc_ref[core, :, 0, bh * half:(bh + 1) * half].reshape(n * half, slots)
                both = jnp.concatenate([direct, mirror], axis=1)
                spread = jnp.dot(both, w_ref[core, h, bh], preferred_element_type=F32)
                spread = spread.astype(BF16).reshape(n, half, width)
                mask = irb[:, bh] == colx_ref[h, :, span][None]
                ebuf[:, bh, :, span] = jnp.where(mask, spread, jnp.zeros_like(spread))
        ladder = lax.dot_general(
            t_ref[...], ebuf[...].reshape(num_virt, 2 * width),
            (((1,), (1,)), ((), ())), preferred_element_type=F32,
        )
        cols = slice(h * num_virt, (h + 1) * num_virt)
        total = res_ref[:, cols].astype(F32) + ladder
        out_ref[:, cols] = (total / (pe_ref[...] - vsum_ref[:, cols])).astype(BF16)


def ranks(column_irrep):
    same = column_irrep[:, None] == column_irrep[None, :]
    index = jnp.arange(column_irrep.shape[0])
    return jnp.sum(same & (index[None, :] < index[:, None]), axis=1, dtype=jnp.int32)


def local(
    amplitudes, integrals, virtual_irrep, column_irrep, pair_energy, virtual_energy, residual_in
):
    n = lax.axis_size("wide")
    num_virt, width = virtual_irrep.shape[0], column_irrep.shape[0]
    al, half = num_virt // n, num_virt // n // 2
    pairs = pair_energy.shape[0]
    me = lax.axis_index("wide")
    first_a = me * al
    local_irrep = lax.dynamic_slice_in_dim(virtual_irrep, first_a, al, 0)

    columns = lax.all_gather(column_irrep, "narrow", axis=0)

    rank = ranks(column_irrep)
    slot = jnp.arange(2 * SLOTS)
    shift = jnp.array([0, SLOTS])[:, None, None]
    inside = (slot >= shift) & (slot < shift + SLOTS)
    pick = ((rank[None, :, None] + shift == slot) & inside).astype(BF16)
    colx = (local_irrep[:, None] ^ column_irrep[None, :]).astype(BF16)[:, None, :]
    irb = jnp.broadcast_to(virtual_irrep.astype(BF16)[:, None], (num_virt, width))

    vmem = pl.BlockSpec(memory_space=pltpu.VMEM)
    hbm = pl.BlockSpec(memory_space=pl.ANY)
    lc, rx, amp = pl.pallas_call(
        functools.partial(exchange_kernel, n),
        out_shape=(
            jax.ShapeDtypeStruct((2, n, half, al, 2 * SLOTS), BF16),
            jax.ShapeDtypeStruct((2, n, al, half, 2 * SLOTS), BF16),
            jax.ShapeDtypeStruct((2, n // 2) + amplitudes.shape, BF16),
        ),
        in_specs=[hbm, vmem, vmem, vmem, vmem],
        out_specs=(hbm, hbm, hbm),
        scratch_shapes=[
            pltpu.VMEM((n, al, al, width), BF16),
            pltpu.VMEM((half * al, 2 * SLOTS), F32),
            pltpu.VMEM((n, al, half, 2 * SLOTS), BF16),
            pltpu.VMEM((n, half, al, 2 * SLOTS), BF16),
            pltpu.VMEM((n,) + amplitudes.shape, BF16),
            pltpu.SemaphoreType.DMA((n,)),
            pltpu.SemaphoreType.DMA((n,)),
            pltpu.SemaphoreType.DMA((3,)),
            pltpu.SemaphoreType.DMA((n,)),
            pltpu.SemaphoreType.DMA((n,)),
            pltpu.SemaphoreType.DMA((n,)),
            pltpu.SemaphoreType.DMA((n,)),
            pltpu.SemaphoreType.DMA((n,)),
            pltpu.SemaphoreType.DMA((2,)),
            pltpu.SemaphoreType.DMA((3,)),
        ],
        compiler_params=pltpu.CompilerParams(
            collective_id=0, has_side_effects=True, vmem_limit_bytes=40 * 2**20
        ),
        cost_estimate=pl.CostEstimate(
            flops=4 * al * num_virt * width * 2 * SLOTS,
            bytes_accessed=200 * 2**20, transcendentals=0,
        ),
    )(integrals.reshape(al, num_virt, width), irb, colx, pick, amplitudes)
    amp = jnp.transpose(amp.reshape(2, pairs, width), (1, 0, 2)).reshape(pairs, 2 * width)

    rank_all = jax.vmap(ranks)(columns)
    fits = jnp.max(rank_all) < SLOTS
    spread = (
        (rank_all[:, None, None, :] + shift[None] == slot[None, None, :, None])
        & jnp.swapaxes(inside, 1, 2)[None]
    )
    spread = spread.astype(BF16)
    shape = (2, 2, 2, 2 * SLOTS, width)
    weights = jnp.concatenate(
        [jnp.broadcast_to(spread[:, :, None], shape), jnp.broadcast_to(-spread[:, None], shape)],
        axis=3,
    )
    colx_all = (local_irrep[:, None] ^ columns.reshape(1, 2 * width)).astype(BF16)[:, None, :]
    local_energy = lax.dynamic_slice_in_dim(virtual_energy, first_a, al, 0)
    vsum = (local_energy[:, None] + virtual_energy[None, :]).reshape(1, al * num_virt)

    def short():
        whole = lambda *shape: pl.BlockSpec(shape, lambda p: (0,) * len(shape))
        return pl.pallas_call(
            finish_kernel,
            grid=(half,),
            out_shape=jax.ShapeDtypeStruct(residual_in.shape, BF16),
            in_specs=[
                pl.BlockSpec((2, n, 1, al, 2 * SLOTS), lambda p: (0, 0, p, 0, 0)),
                pl.BlockSpec((2, n, 2, half, 2 * SLOTS), lambda p: (0, 0, p, 0, 0)),
                whole(2, 2, 2, 4 * SLOTS, width),
                whole(pairs, 2 * width),
                pl.BlockSpec((2, 1, 2 * width), lambda p: (p, 0, 0)),
                whole(num_virt, width),
                pl.BlockSpec((pairs, 2 * num_virt), lambda p: (0, p)),
                whole(pairs, 1),
                pl.BlockSpec((1, 2 * num_virt), lambda p: (0, p)),
            ],
            out_specs=pl.BlockSpec((pairs, 2 * num_virt), lambda p: (0, p)),
            scratch_shapes=[pltpu.VMEM((n, 2, half, 2 * width), BF16)],
            compiler_params=pltpu.CompilerParams(vmem_limit_bytes=40 * 2**20),
        )(lc, rx, weights, amp, colx_all, irb, residual_in, pair_energy[:, None], vsum)

    def full():
        return dense(
            amplitudes, integrals, virtual_irrep, column_irrep, pair_energy, virtual_energy,
            residual_in,
        )

    return lax.cond(fits, short, full)


def solution(mesh):
    usable = mesh.shape["narrow"] == 2 and mesh.shape["wide"] == 16
    return jax.shard_map(
        local if usable else dense,
        mesh=mesh,
        in_specs=(
            P("wide", "narrow"),
            P("wide", "narrow"),
            P(),
            P("narrow"),
            P("narrow"),
            P(),
            P("narrow", "wide"),
        ),
        out_specs=P("narrow", "wide"),
        check_vma=False,
    )
```

```python
import functools

import jax
import jax.numpy as jnp
from jax import lax
from jax.experimental import pallas as pl
from jax.experimental.pallas import tpu as pltpu
from jax.sharding import PartitionSpec as P

SLOTS = 64
MESH = pl.DeviceIdType.MESH
BF16 = jnp.bfloat16
F32 = jnp.float32


def dense(
    amplitudes, integrals, virtual_irrep, column_irrep, pair_energy, virtual_energy, residual_in
):
    wide_size = lax.axis_size("wide")
    num_virt = virtual_irrep.shape[0]
    a_local = num_virt // wide_size
    first_a = lax.axis_index("wide") * a_local
    local_irrep = lax.dynamic_slice_in_dim(virtual_irrep, first_a, a_local, 0)
    row_irrep = jnp.bitwise_xor(local_irrep[:, None], virtual_irrep[None, :]).reshape(
        a_local * num_virt
    )
    masked = jnp.where(
        row_irrep[:, None] == column_irrep[None, :], integrals, jnp.zeros((), integrals.dtype)
    )
    contract = (((1,), (1,)), ((), ()))
    terms = lax.dot_general(
        lax.all_gather(amplitudes, "wide", axis=0, tiled=True),
        masked,
        contract,
        preferred_element_type=jnp.float32,
    )
    ladder = lax.psum_scatter(
        terms.astype(jnp.bfloat16), "narrow", scatter_dimension=0, tiled=True
    ).astype(jnp.float32)
    pair_rows = ladder.shape[0]
    ladder_cube = ladder.reshape(pair_rows, a_local, num_virt)
    swapped = lax.all_to_all(
        ladder_cube.astype(jnp.bfloat16), "wide", split_axis=2, concat_axis=2, tiled=True
    ).astype(ladder_cube.dtype)
    mirrored = swapped.reshape(pair_rows, a_local, wide_size, a_local)
    mirrored = jnp.transpose(mirrored, (0, 3, 2, 1)).reshape(pair_rows, a_local * num_virt)
    local_energy = lax.dynamic_slice_in_dim(virtual_energy, first_a, a_local, 0)
    denominator = (
        pair_energy[:, None, None] - local_energy[None, :, None] - virtual_energy[None, None, :]
    )
    denominator = denominator.reshape(pair_rows, a_local * num_virt)
    total = residual_in.astype(jnp.float32) + ladder - mirrored
    return (total / denominator).astype(jnp.bfloat16)


def partner(me, step, n):
    result, bit = 0, 1
    while bit < n:
        result += ((me // bit + step // bit) % 2) * bit
        bit *= 2
    return result


def exchange_kernel(
    n, v_ref, irb_ref, colx_ref, s_ref, amp_ref, lc_ref, rx_ref, t_ref,
    vbuf, fbuf, tx, lcbuf, tbuf, tsend_sem, trecv_sem, tgive_sem, load_sem, send_sem, recv_sem, fsend_sem, frecv_sem, own_sem, lc_sem,
):
    me, core = lax.axis_index("wide"), lax.axis_index("narrow")
    other = 1 - core
    al = v_ref.shape[0]
    half = al // 2
    width = v_ref.shape[2]

    def load(i):
        to = partner(me, i + 1, n)
        columns = pl.ds(pl.multiple_of(to * al, al), al)
        return pltpu.make_async_copy(v_ref.at[:, columns, :], vbuf.at[i], load_sem.at[i])

    def send(i):
        to = partner(me, i + 1, n)
        return pltpu.make_async_remote_copy(
            src_ref=tx.at[i], dst_ref=rx_ref.at[core, me], send_sem=send_sem.at[i],
            recv_sem=recv_sem.at[i], device_id=(to, core), device_id_type=MESH,
        )

    def arrival(i):
        source = partner(me, i + 1, n)
        return pltpu.make_async_remote_copy(
            src_ref=tx.at[i], dst_ref=rx_ref.at[core, source], send_sem=send_sem.at[i],
            recv_sem=recv_sem.at[i], device_id=(source, core), device_id_type=MESH,
        )

    def forward(i):
        source = partner(me, i + 1, n)
        return pltpu.make_async_remote_copy(
            src_ref=rx_ref.at[core, source], dst_ref=rx_ref.at[core, source],
            send_sem=fsend_sem.at[i], recv_sem=frecv_sem.at[i],
            device_id=(me, other), device_id_type=MESH,
        )

    def forwarded(i):
        source = partner(me, i + 1, n)
        return pltpu.make_async_remote_copy(
            src_ref=rx_ref.at[other, source], dst_ref=rx_ref.at[other, source],
            send_sem=fsend_sem.at[i], recv_sem=frecv_sem.at[i],
            device_id=(me, other), device_id_type=MESH,
        )

    def send_amp(i):
        return pltpu.make_async_remote_copy(
            src_ref=amp_ref, dst_ref=tbuf.at[me], send_sem=tsend_sem.at[i],
            recv_sem=trecv_sem.at[i], device_id=(partner(me, i + 1, n), core),
            device_id_type=MESH,
        )

    def arrived_amp(i):
        source = partner(me, i + 1, n)
        return pltpu.make_async_remote_copy(
            src_ref=amp_ref, dst_ref=tbuf.at[source], send_sem=tsend_sem.at[i],
            recv_sem=trecv_sem.at[i], device_id=(source, core), device_id_type=MESH,
        )

    barrier = pltpu.get_barrier_semaphore()

    @pl.loop(0, n - 1)
    def _(i):
        pl.semaphore_signal(
            barrier, inc=1, device_id=(partner(me, i + 1, n), core), device_id_type=MESH
        )

    pl.semaphore_signal(barrier, inc=1, device_id=(me, other), device_id_type=MESH)

    @pl.loop(0, n)
    def _(i):
        load(i).start()

    own_amp = pltpu.make_async_copy(amp_ref, tbuf.at[me], own_sem.at[1])
    own_amp.start()
    pl.semaphore_wait(barrier, n)

    @pl.loop(0, n - 1)
    def _(i):
        send_amp(i).start()

    @pl.loop(0, n)
    def _(i):
        to = partner(me, i + 1, n)
        load(i).wait()
        rows = irb_ref[pl.ds(pl.multiple_of(to * al, al), al), :]
        block = vbuf[i]
        masked = jnp.where(rows[None] == colx_ref[...], block, jnp.zeros_like(block))
        low, high = s_ref[0], s_ref[1]

        def pack(first, second):
            return jnp.dot(
                first.reshape(half * al, width), low, preferred_element_type=F32
            ) + jnp.dot(second.reshape(half * al, width), high, preferred_element_type=F32)

        fbuf[...] = pack(masked[:half], masked[half:])
        pairs = masked.reshape(half, 2, al, width)
        lcbuf[to] = pack(pairs[:, 0], pairs[:, 1]).astype(BF16).reshape(half, al, 2 * SLOTS)
        for b in range(al):
            tx[i, b] = fbuf[pl.ds(b, half, stride=al), :].astype(BF16)

        @pl.when(i < n - 1)
        def _():
            send(i).start()

    own = pltpu.make_async_copy(tx.at[n - 1], rx_ref.at[core, me], own_sem.at[0])
    own.start()
    keep = pltpu.make_async_copy(lcbuf, lc_ref.at[core], lc_sem.at[0])
    keep.start()
    give = pltpu.make_async_remote_copy(
        src_ref=lcbuf, dst_ref=lc_ref.at[core], send_sem=lc_sem.at[1], recv_sem=lc_sem.at[2],
        device_id=(me, other), device_id_type=MESH,
    )
    give.start()
    own.wait()
    forward(n - 1).start()
    own_amp.wait()

    @pl.loop(0, n - 1)
    def _(i):
        arrived_amp(i).wait_recv()

    keep_amp = pltpu.make_async_copy(
        tbuf.at[pl.ds(core * (n // 2), n // 2)], t_ref.at[core], tgive_sem.at[0]
    )
    keep_amp.start()
    give_amp = pltpu.make_async_remote_copy(
        src_ref=tbuf.at[pl.ds(other * (n // 2), n // 2)], dst_ref=t_ref.at[core],
        send_sem=tgive_sem.at[1], recv_sem=tgive_sem.at[2],
        device_id=(me, other), device_id_type=MESH,
    )
    give_amp.start()

    @pl.loop(0, n - 1)
    def _(i):
        arrival(i).wait_recv()
        forward(i).start()

    @pl.loop(0, n - 1)
    def _(i):
        send(i).wait_send()
        send_amp(i).wait_send()

    @pl.loop(0, n)
    def _(i):
        forward(i).wait_send()
        forwarded(i).wait_recv()

    keep_amp.wait()
    give_amp.wait_send()
    pltpu.make_async_remote_copy(
        src_ref=tbuf.at[pl.ds(other * (n // 2), n // 2)], dst_ref=t_ref.at[other],
        send_sem=tgive_sem.at[1], recv_sem=tgive_sem.at[2],
        device_id=(me, other), device_id_type=MESH,
    ).wait_recv()
    keep.wait()
    give.wait_send()
    pltpu.make_async_remote_copy(
        src_ref=lcbuf, dst_ref=lc_ref.at[other], send_sem=lc_sem.at[1], recv_sem=lc_sem.at[2],
        device_id=(me, other), device_id_type=MESH,
    ).wait_recv()


def finish_kernel(
    lc_ref, rx_ref, w_ref, t_ref, colx_ref, irb_ref, res_ref, pe_ref, vsum_ref, out_ref, ebuf
):
    n, half, slots = rx_ref.shape[1], rx_ref.shape[3], rx_ref.shape[4]
    width = irb_ref.shape[1]
    num_virt = irb_ref.shape[0]
    irb = irb_ref[...].reshape(n, 2, half, width)
    for h in range(2):
        for core in range(2):
            mirror = rx_ref[core, :, h].reshape(n * half, slots)
            span = slice(core * width, (core + 1) * width)
            for bh in range(2):
                direct = lc_ref[core, :, 0, bh * half:(bh + 1) * half].reshape(n * half, slots)
                both = jnp.concatenate([direct, mirror], axis=1)
                spread = jnp.dot(both, w_ref[core, h, bh], preferred_element_type=F32)
                spread = spread.astype(BF16).reshape(n, half, width)
                mask = irb[:, bh] == colx_ref[h, :, span][None]
                ebuf[:, bh, :, span] = jnp.where(mask, spread, jnp.zeros_like(spread))
        ladder = lax.dot_general(
            t_ref[...], ebuf[...].reshape(num_virt, 2 * width),
            (((1,), (1,)), ((), ())), preferred_element_type=F32,
        )
        cols = slice(h * num_virt, (h + 1) * num_virt)
        total = res_ref[:, cols].astype(F32) + ladder
        out_ref[:, cols] = (total / (pe_ref[...] - vsum_ref[:, cols])).astype(BF16)


def ranks(column_irrep):
    same = column_irrep[:, None] == column_irrep[None, :]
    index = jnp.arange(column_irrep.shape[0])
    return jnp.sum(same & (index[None, :] < index[:, None]), axis=1, dtype=jnp.int32)


def local(
    amplitudes, integrals, virtual_irrep, column_irrep, pair_energy, virtual_energy, residual_in
):
    n = lax.axis_size("wide")
    num_virt, width = virtual_irrep.shape[0], column_irrep.shape[0]
    al, half = num_virt // n, num_virt // n // 2
    pairs = pair_energy.shape[0]
    me = lax.axis_index("wide")
    first_a = me * al
    local_irrep = lax.dynamic_slice_in_dim(virtual_irrep, first_a, al, 0)

    columns = lax.all_gather(column_irrep, "narrow", axis=0)

    rank = ranks(column_irrep)
    slot = jnp.arange(2 * SLOTS)
    shift = jnp.array([0, SLOTS])[:, None, None]
    inside = (slot >= shift) & (slot < shift + SLOTS)
    pick = ((rank[None, :, None] + shift == slot) & inside).astype(BF16)
    colx = (local_irrep[:, None] ^ column_irrep[None, :]).astype(BF16)[:, None, :]
    irb = jnp.broadcast_to(virtual_irrep.astype(BF16)[:, None], (num_virt, width))

    vmem = pl.BlockSpec(memory_space=pltpu.VMEM)
    hbm = pl.BlockSpec(memory_space=pl.ANY)
    lc, rx, amp = pl.pallas_call(
        functools.partial(exchange_kernel, n),
        out_shape=(
            jax.ShapeDtypeStruct((2, n, half, al, 2 * SLOTS), BF16),
            jax.ShapeDtypeStruct((2, n, al, half, 2 * SLOTS), BF16),
            jax.ShapeDtypeStruct((2, n // 2) + amplitudes.shape, BF16),
        ),
        in_specs=[hbm, vmem, vmem, vmem, vmem],
        out_specs=(hbm, hbm, hbm),
        scratch_shapes=[
            pltpu.VMEM((n, al, al, width), BF16),
            pltpu.VMEM((half * al, 2 * SLOTS), F32),
            pltpu.VMEM((n, al, half, 2 * SLOTS), BF16),
            pltpu.VMEM((n, half, al, 2 * SLOTS), BF16),
            pltpu.VMEM((n,) + amplitudes.shape, BF16),
            pltpu.SemaphoreType.DMA((n,)),
            pltpu.SemaphoreType.DMA((n,)),
            pltpu.SemaphoreType.DMA((3,)),
            pltpu.SemaphoreType.DMA((n,)),
            pltpu.SemaphoreType.DMA((n,)),
            pltpu.SemaphoreType.DMA((n,)),
            pltpu.SemaphoreType.DMA((n,)),
            pltpu.SemaphoreType.DMA((n,)),
            pltpu.SemaphoreType.DMA((2,)),
            pltpu.SemaphoreType.DMA((3,)),
        ],
        compiler_params=pltpu.CompilerParams(
            collective_id=0, has_side_effects=True, vmem_limit_bytes=40 * 2**20
        ),
        cost_estimate=pl.CostEstimate(
            flops=4 * al * num_virt * width * 2 * SLOTS,
            bytes_accessed=200 * 2**20, transcendentals=0,
        ),
    )(integrals.reshape(al, num_virt, width), irb, colx, pick, amplitudes)
    amp = jnp.transpose(amp.reshape(2, pairs, width), (1, 0, 2)).reshape(pairs, 2 * width)

    rank_all = jax.vmap(ranks)(columns)
    fits = jnp.max(rank_all) < SLOTS
    spread = (
        (rank_all[:, None, None, :] + shift[None] == slot[None, None, :, None])
        & jnp.swapaxes(inside, 1, 2)[None]
    )
    spread = spread.astype(BF16)
    shape = (2, 2, 2, 2 * SLOTS, width)
    weights = jnp.concatenate(
        [jnp.broadcast_to(spread[:, :, None], shape), jnp.broadcast_to(-spread[:, None], shape)],
        axis=3,
    )
    colx_all = (local_irrep[:, None] ^ columns.reshape(1, 2 * width)).astype(BF16)[:, None, :]
    local_energy = lax.dynamic_slice_in_dim(virtual_energy, first_a, al, 0)
    vsum = (local_energy[:, None] + virtual_energy[None, :]).reshape(1, al * num_virt)

    def short():
        whole = lambda *shape: pl.BlockSpec(shape, lambda p: (0,) * len(shape))
        return pl.pallas_call(
            finish_kernel,
            grid=(half,),
            out_shape=jax.ShapeDtypeStruct(residual_in.shape, BF16),
            in_specs=[
                pl.BlockSpec((2, n, 1, al, 2 * SLOTS), lambda p: (0, 0, p, 0, 0)),
                pl.BlockSpec((2, n, 2, half, 2 * SLOTS), lambda p: (0, 0, p, 0, 0)),
                whole(2, 2, 2, 4 * SLOTS, width),
                whole(pairs, 2 * width),
                pl.BlockSpec((2, 1, 2 * width), lambda p: (p, 0, 0)),
                whole(num_virt, width),
                pl.BlockSpec((pairs, 2 * num_virt), lambda p: (0, p)),
                whole(pairs, 1),
                pl.BlockSpec((1, 2 * num_virt), lambda p: (0, p)),
            ],
            out_specs=pl.BlockSpec((pairs, 2 * num_virt), lambda p: (0, p)),
            scratch_shapes=[pltpu.VMEM((n, 2, half, 2 * width), BF16)],
            compiler_params=pltpu.CompilerParams(vmem_limit_bytes=40 * 2**20),
        )(lc, rx, weights, amp, colx_all, irb, residual_in, pair_energy[:, None], vsum)

    def full():
        return dense(
            amplitudes, integrals, virtual_irrep, column_irrep, pair_energy, virtual_energy,
            residual_in,
        )

    return lax.cond(fits, short, full)


def solution(mesh):
    usable = mesh.shape["narrow"] == 2 and mesh.shape["wide"] == 16
    return jax.shard_map(
        local if usable else dense,
        mesh=mesh,
        in_specs=(
            P("wide", "narrow"),
            P("wide", "narrow"),
            P(),
            P("narrow"),
            P("narrow"),
            P(),
            P("narrow", "wide"),
        ),
        out_specs=P("narrow", "wide"),
        check_vma=False,
    )
```
